32 devices in a mesh: band: 4 (over z), gy: 8 (over y, x, core).
Axes of the slice: x: 2, y: 2, z: 4, core: 2. Of those that a mesh axis runs over, the one named last changes fastest.
Arguments:
- orbitals: float32 [16, 32, 512, 256], P('band', None, 'gy'), may hold values from -11 to 11
- potentials: float32 [2, 32, 512, 256], P(None, None, 'gy'), may hold values from -1 to 3
- local_potential: float32 [32, 512, 256], P(None, 'gy'), may hold values from 0 to 1
- shifts: float32 [16], P('band'), may hold values from 0.05 to 0.8
Outputs:
- field_response: float32 [2, 32, 256, 512], P(None, 'band', 'gy')
The draws below stay inside these ranges and needn't reach their ends.
All inputs are finite; a program needn't handle non-finite values.
Results may differ from the reference program's by a relative error of at most 0.0003.
Values sent between devices are 32-bit elements; how exact they have to be, the bound alone decides.
No kernel may reach another device: no remote copies, remote signals or barrier semaphores. Data moves between devices by JAX's collectives and lax.ppermute only.
A program may use at most 256 MiB of HBM per device.

```python
import math
import jax
import jax.numpy as jnp
from jax import lax

NX = 256
NY = 512
NZ = 32
NPOT = 2
SWEEPS = 3
NORB = 16


def draw_orbitals(key, part):
    rows = jnp.arange(NY, dtype=jnp.float32) / (NY - 1)
    values = jax.random.truncated_normal(key, -6.0, 6.0, (NORB, NZ, NY, NX), jnp.float32)
    envelope = jnp.sqrt(1.0 + 2.0 * rows)
    return values * envelope[None, None, :, None]


def draw_potentials(key, part):
    values = 1.0 + 0.5 * jax.random.truncated_normal(key, -4.0, 4.0, (NPOT, NZ, NY, NX), jnp.float32)
    return values


def steps_of(own_key, dims, cuts, least, top_value):
    def one(position, parts):
        heights = jax.random.uniform(jax.random.fold_in(jax.random.fold_in(own_key, 6), position), (parts,), jnp.float32, least / len(cuts), top_value / len(cuts))
        return jnp.repeat(jnp.exp(heights), dims[position] // parts).reshape((-1,) + (1,) * (len(dims) - position - 1))

    level = one(*cuts[0])
    for cut in cuts[1:]:
        level = level * one(*cut)
    return level


def setup_inputs(seed: int = 0) -> dict:
    keys = jax.random.split(jax.random.key(seed), 5)
    return {
        "orbitals": draw_orbitals(jax.random.fold_in(keys[4], 71), 0),
        "potentials": draw_potentials(jax.random.fold_in(keys[4], 71), 0),
        "local_potential": jnp.clip(1.0 * jax.random.uniform(keys[2], (NZ, NY, NX), jnp.float32) ** steps_of(keys[2], (NZ, NY, NX), ((1, 8),), -0.2, 0.2), 0.0, 1.0),
        "shifts": jnp.clip(jnp.exp(math.log(0.8) - 2.7725887 * jax.random.uniform(keys[3], (NORB,), jnp.float32) ** steps_of(keys[3], (NORB,), ((0, 4),), -0.2, 0.2)), 0.05, 0.8),
    }


spread_half = 3.5
screening = 0.25

def sine_table(length):
    index = jnp.arange(1, length + 1, dtype=jnp.int32)
    phase = index[:, None] * index[None, :] % (2 * (length + 1))
    scale = jnp.sqrt(jnp.float32(2.0) / (length + 1))
    return scale * jnp.sin(jnp.float32(jnp.pi) * phase.astype(jnp.float32) / (length + 1))

def coulomb(z_index, x_index, y_index):
    wave_z = jnp.pi * (z_index.astype(jnp.float32) + 1.0) / (NZ + 1)
    wave_x = jnp.pi * (x_index.astype(jnp.float32) + 1.0) / (NX + 1)
    wave_y = jnp.pi * (y_index.astype(jnp.float32) + 1.0) / (NY + 1)
    total = wave_z[:, None, None] * wave_z[:, None, None] + wave_x[None, :, None] * wave_x[None, :, None]
    total = total + wave_y[None, None, :] * wave_y[None, None, :] + screening
    return jnp.sqrt(4.0 * jnp.pi / total)

def beside(field, axis):
    size = field.shape[axis]
    upper = lax.slice_in_dim(field, 1, size, axis=axis)
    lower = lax.slice_in_dim(field, 0, size - 1, axis=axis)
    pad_upper = tuple(((0, 1) if i == axis else (0, 0) for i in range(field.ndim)))
    pad_lower = tuple(((1, 0) if i == axis else (0, 0) for i in range(field.ndim)))
    return jnp.pad(upper, pad_upper) + jnp.pad(lower, pad_lower)

def pad_rows(field):
    return jnp.pad(field, tuple(((1, 1) if i == field.ndim - 2 else (0, 0) for i in range(field.ndim))))

def operate(padded, local_potential, shift):
    center = padded[..., 1:-1, :]
    near = padded[..., 2:, :] + padded[..., :-2, :]
    near = near + beside(center, center.ndim - 1) + beside(center, center.ndim - 3)
    return (3.0 + local_potential + shift) * center - 0.5 * near

def chebyshev(source, apply_fn, shift):
    center_value = shift + spread_half
    ratio_start = center_value / spread_half
    weight_now = 1.0 / ratio_start
    direction = source / center_value
    residual = source
    iterate = jnp.zeros_like(source)
    for sweep in range(SWEEPS):
        iterate = iterate + direction
        residual = residual - apply_fn(direction)
        weight_next = 1.0 / (2.0 * ratio_start - weight_now)
        direction = weight_next * weight_now * direction + 2.0 * weight_next / spread_half * residual
        weight_now = weight_next
    return iterate + direction

def reference(orbitals, potentials, local_potential, shifts):

    def one_orbital(density, item):
        orbital, shift = item
        squares = orbital * orbital
        coefficient = lax.optimization_barrier(jnp.sum(potentials * squares[None], axis=(1, 2, 3))) / jnp.sum(squares)
        source = (potentials - coefficient[:, None, None, None]) * orbital[None]

        def apply_fn(field):
            return operate(pad_rows(field), local_potential, shift)
        response = chebyshev(source, apply_fn, shift)
        return (density - 4.0 * orbital[None] * response, None)
    density = lax.scan(one_orbital, jnp.zeros(potentials.shape, jnp.float32), (orbitals, shifts))[0]
    highest = lax.Precision.HIGHEST
    along_z = jnp.einsum('kz,pzyx->pkyx', sine_table(NZ), density, precision=highest)
    along_x = jnp.einsum('jx,pkyx->pkyj', sine_table(NX), along_z, precision=highest)
    along_y = jnp.einsum('my,pkyj->pkjm', sine_table(NY), along_x, precision=highest)
    weight = coulomb(jnp.arange(NZ, dtype=jnp.int32), jnp.arange(NX, dtype=jnp.int32), jnp.arange(NY, dtype=jnp.int32))
    return along_y * weight[None]
```

```python
import functools

import jax
import jax.numpy as jnp
import numpy as np
from jax import lax
from jax.experimental import pallas as pl
from jax.experimental.pallas import tpu as pltpu
from jax.sharding import PartitionSpec as P

SWEEPS = 3
HALO = SWEEPS
TILE = 8
LANES = 128

spread_half = 3.5
screening = 0.25


def sine_values(length):
    index = np.arange(1, length + 1)
    phase = index[:, None] * index[None, :] % (2 * (length + 1))
    return np.sqrt(2.0 / (length + 1)) * np.sin(np.pi * phase / (length + 1))


def two_parts(values):
    whole = np.asarray(values, np.float32)
    high = whole.astype(jnp.bfloat16)
    low = (whole - high.astype(np.float32)).astype(jnp.bfloat16)
    return np.stack([high, low])


def split(value):
    high = value.astype(jnp.bfloat16)
    low = (value - high.astype(jnp.float32)).astype(jnp.bfloat16)
    return high, low


def product(a, b, contract):
    dims = (contract, ((), ()))
    dot = functools.partial(lax.dot_general, dimension_numbers=dims, preferred_element_type=jnp.float32)
    return dot(a[0], b[0]) + dot(a[1], b[0]) + dot(a[0], b[1])


def coulomb(z_index, x_index, y_index, sizes):
    nz, nx, ny = sizes
    wave_z = jnp.pi * (z_index.astype(jnp.float32) + 1.0) / (nz + 1)
    wave_x = jnp.pi * (x_index.astype(jnp.float32) + 1.0) / (nx + 1)
    wave_y = jnp.pi * (y_index.astype(jnp.float32) + 1.0) / (ny + 1)
    total = (
        wave_z[:, None, None] * wave_z[:, None, None]
        + wave_x[None, :, None] * wave_x[None, :, None]
    )
    total = total + wave_y[None, None, :] * wave_y[None, None, :] + screening
    return jnp.sqrt(4.0 * jnp.pi / total)


def project_kernel(orbitals, potentials, out):
    count, planes, rows, width = orbitals.shape
    npot = potentials.shape[0]
    halves = width // LANES

    @pl.when(pl.program_id(0) == 0)
    def _():
        out[...] = jnp.zeros_like(out)

    def fold(value):
        return jnp.sum(value.reshape(rows // TILE, TILE, LANES), axis=0)

    def body(z, _):
        for half in range(halves):
            lanes = slice(half * LANES, (half + 1) * LANES)
            potential = [potentials[p, z, :, lanes] for p in range(npot)]
            for n in range(count):
                value = orbitals[n, z, :, lanes]
                square = value * value
                for p in range(npot):
                    out[p * count + n] += fold(potential[p] * square)
                out[npot * count + n] += fold(square)
        return 0

    lax.fori_loop(0, planes, body, 0)


def project(orbitals, potentials):
    count, planes, rows, width = orbitals.shape
    npot = potentials.shape[0]
    step = 4
    sums = (npot + 1) * count
    partial_sums = pl.pallas_call(
        project_kernel,
        grid=(planes // step,),
        in_specs=[
            pl.BlockSpec((count, step, rows, width), lambda i: (0, i, 0, 0)),
            pl.BlockSpec((npot, step, rows, width), lambda i: (0, i, 0, 0)),
        ],
        out_specs=pl.BlockSpec((sums, TILE, LANES), lambda i: (0, 0, 0)),
        out_shape=jax.ShapeDtypeStruct((sums, TILE, LANES), jnp.float32),
        compiler_params=pltpu.CompilerParams(vmem_limit_bytes=40 << 20),
    )(orbitals, potentials)
    return jnp.sum(partial_sums, axis=1)


def stencil_kernel(
    geometry,
    sums, constants, edges, z_table, x_table, neighbours,
    orbitals, potentials, local, low, high,
    mine, partner, far,
    orb, pot, loc, src, one, two, density, spectrum, sems,
):
    first_p, npot, all_pots, count, start, rows, strip, group = geometry
    planes = local.shape[0]
    width = local.shape[2]
    halves = width // LANES
    padded = rows + 2 * TILE
    f32 = jnp.float32

    begin, end = max(start - TILE, 0), min(start + rows + TILE, strip)
    place = begin - (start - TILE)
    copies = {}
    slot = 0
    fields = [("loc", 0, local, None, loc, all_pots + count)]
    for p in range(npot):
        fields.append(("pot", p, potentials, first_p + p, pot, count + first_p + p))
    for n in range(count):
        fields.append(("orb", n, orbitals, n, orb, n))
    for name, position, source, index, target, halo_index in fields:
        started = []
        for half in range(halves):
            lanes = pl.ds(half * LANES, LANES)
            whole = source if index is None else source.at[index]
            into = target.at[half] if index is None else target.at[half, position]
            pieces = [(whole.at[:, pl.ds(begin, end - begin), lanes], into.at[:, pl.ds(place, end - begin), :])]
            if start - TILE < 0:
                pieces.append((low.at[halo_index, :, :, lanes], into.at[:, pl.ds(0, TILE), :]))
            if start + rows + TILE > strip:
                pieces.append((high.at[halo_index, :, :, lanes], into.at[:, pl.ds(padded - TILE, TILE), :]))
            for a, b in pieces:
                copy = pltpu.make_async_copy(a, b, sems.at[slot])
                copy.start()
                started.append(copy)
                slot += 1
        copies[name, position] = started

    def wait(name, position):
        for copy in copies[name, position]:
            copy.wait()

    for field in (src, one, two):
        for half in range(halves):
            for z in (0, planes + 1):
                field[half, z] = jnp.zeros(field.shape[2:], f32)

    totals = jnp.sum(sums[...], axis=1, keepdims=True)
    first_edge, last_edge = edges[0] == 1, edges[1] == 1
    if start > 0:
        first_edge = None
    if start + rows < strip:
        last_edge = None
    band_matrix = neighbours[...]

    wait("loc", 0)

    def weights(z, _):
        for half in range(halves):
            loc[half, z] = 1.0 - 2.0 * loc[half, z]
        return 0

    lax.fori_loop(0, planes, weights, 0)

    def apply(field, offset, size, loc_offset, finish):
        def body(step, _):
            z0 = step * group
            centers = []
            for i in range(group):
                centers.append([field[h, z0 + i + 1, pl.ds(offset, size), :] for h in range(halves)])
            joined = jnp.concatenate([jnp.concatenate(c, axis=-1) for c in centers], axis=0)
            upper, lower = split(joined)
            near = jnp.dot(upper, band_matrix, preferred_element_type=f32)
            near = near + jnp.dot(lower, band_matrix, preferred_element_type=f32)
            for i in range(group):
                z = z0 + i
                for h in range(halves):
                    total = near[i * size:(i + 1) * size, h * LANES:(h + 1) * LANES]
                    total = total + (field[h, z + 1, pl.ds(offset - 1, size), :] + field[h, z + 1, pl.ds(offset + 1, size), :])
                    total = total + (field[h, z, pl.ds(offset, size), :] + field[h, z + 2, pl.ds(offset, size), :])
                    finish(z, h, total, centers[i][h], loc[h, z, pl.ds(loc_offset, size), :])
            return 0

        lax.fori_loop(0, planes // group, body, 0)

    def clear(field, where, row, size):
        if where is not None:
            @pl.when(where)
            def _():
                for h in range(halves):
                    field[h, :, pl.ds(row, size), :] = jnp.zeros((planes + 2, size, LANES), f32)

    for n in range(count):
        wait("orb", n)
        square, linear, constant, scale = (constants[n, i] for i in range(4))
        for p in range(npot):
            if n == 0:
                wait("pot", p)
            pair = (first_p + p) * count + n
            norm = all_pots * count + n
            coefficient = totals[pair:pair + 1] / totals[norm:norm + 1]

            def source(z, _):
                for h in range(halves):
                    src[h, z + 1] = (pot[h, p, z] - coefficient) * orb[h, n, z]
                return 0

            lax.fori_loop(0, planes, source, 0)

            def finish_one(z, h, near, center, weight):
                one[h, z + 1, pl.ds(0, rows + TILE), :] = near + (weight + square) * center

            apply(src, TILE - 2, rows + TILE, TILE - 2, finish_one)
            clear(one, first_edge, 0, 2)
            clear(one, last_edge, rows + 2, 2)

            def finish_two(z, h, near, center, weight):
                two[h, z + 1] = near + weight * center + linear * src[h, z + 1, pl.ds(TILE - 1, rows + TILE), :]

            apply(one, 1, rows + TILE, TILE - 1, finish_two)
            clear(two, first_edge, 0, 1)
            clear(two, last_edge, rows + 1, 1)

            def finish_three(z, h, near, center, weight):
                value = near + weight * center + constant * src[h, z + 1, pl.ds(TILE, rows), :]
                value = value * (orb[h, n, z, pl.ds(TILE, rows), :] * scale)
                if n > 0:
                    value = value + density[h, p, z]
                density[h, p, z] = value

            apply(two, 1, rows, TILE, finish_three)

    z_parts = (z_table[0], z_table[1])
    x_parts = (x_table[0], x_table[1])
    share = mine.shape[2]
    block = min(share, 2 * LANES)
    for p in range(npot):
        for tile in range(rows // TILE):
            span = pl.ds(tile * TILE, TILE)
            value = jnp.concatenate(
                [density[h, p, :, span, :].reshape(planes * TILE, LANES) for h in range(halves)], axis=-1
            )
            value = product(z_parts, split(value), ((1,), (0,)))
            spectrum[:, span, :] = value.reshape(planes, TILE, width)
        for piece in range(planes * rows // block):
            at = piece * block
            value = spectrum[at // rows:(at + block) // rows].reshape(block, width)
            value = product(x_parts, split(value), ((1,), (1,)))
            if at < share:
                mine[p, :, at:at + block] = value
            elif at < 2 * share:
                partner[p, :, at - share:at - share + block] = value
            else:
                far[p, :, at - 2 * share:at - 2 * share + block] = value


def stencil(first_p, npot, start, rows, group, sums, constants, edges, tables, fields, halos):
    orbitals, potentials, local = fields
    count, planes, strip, width = orbitals.shape
    all_pots = potentials.shape[0]
    halves = width // LANES
    padded = rows + 2 * TILE
    share = planes * rows // 4
    geometry = (first_p, npot, all_pots, count, start, rows, strip, group)
    vmem = pl.BlockSpec(memory_space=pltpu.VMEM)
    smem = pl.BlockSpec(memory_space=pltpu.SMEM)
    anywhere = pl.BlockSpec(memory_space=pl.ANY)
    f32 = jnp.float32
    return pl.pallas_call(
        functools.partial(stencil_kernel, geometry),
        in_specs=[vmem, smem, smem, vmem, vmem, vmem] + [anywhere] * 5,
        out_specs=[vmem] * 3,
        out_shape=[
            jax.ShapeDtypeStruct((npot, width, share), f32),
            jax.ShapeDtypeStruct((npot, width, share), f32),
            jax.ShapeDtypeStruct((npot, width, 2 * share), f32),
        ],
        scratch_shapes=[
            pltpu.VMEM((halves, count, planes, padded, LANES), f32),
            pltpu.VMEM((halves, npot, planes, padded, LANES), f32),
            pltpu.VMEM((halves, planes, padded, LANES), f32),
            pltpu.VMEM((halves, planes + 2, padded, LANES), f32),
            pltpu.VMEM((halves, planes + 2, padded, LANES), f32),
            pltpu.VMEM((halves, planes + 2, rows + TILE, LANES), f32),
            pltpu.VMEM((halves, npot, planes, rows, LANES), f32),
            pltpu.VMEM((planes, rows, width), f32),
            pltpu.SemaphoreType.DMA(((1 + npot + count) * halves * 3,)),
        ],
        compiler_params=pltpu.CompilerParams(vmem_limit_bytes=56 << 20),
    )(sums, constants, edges, *tables, orbitals, potentials, local, *halos)


def finish_kernel(received, table, weight, out):
    parts, x_share, lanes = received.shape
    z_share = out.shape[0]
    strip = lanes // z_share
    table_parts = (table[0], table[1])
    lane = lax.broadcasted_iota(jnp.int32, (x_share, LANES), 1)
    lower = lane < strip
    for pair in range(z_share // 2):
        columns = slice(pair * LANES, (pair + 1) * LANES)
        blocks = [received[i, :, columns] for i in range(parts)]
        rolled = [pltpu.roll(b, strip, 1) for b in blocks]
        even = [jnp.where(lower, blocks[i], rolled[i + 1]) for i in range(0, parts, 2)]
        odd = [jnp.where(lower, rolled[i], blocks[i + 1]) for i in range(0, parts, 2)]
        both = jnp.concatenate([jnp.concatenate(even, axis=-1), jnp.concatenate(odd, axis=-1)], axis=0)
        value = product(split(both), table_parts, ((1,), (0,)))
        out[2 * pair] = value[:x_share] * weight[2 * pair]
        out[2 * pair + 1] = value[x_share:] * weight[2 * pair + 1]


def finish(received, table, weight):
    vmem = pl.BlockSpec(memory_space=pltpu.VMEM)
    return pl.pallas_call(
        finish_kernel,
        in_specs=[vmem] * 3,
        out_specs=vmem,
        out_shape=jax.ShapeDtypeStruct(weight.shape, jnp.float32),
        compiler_params=pltpu.CompilerParams(vmem_limit_bytes=40 << 20),
    )(received, table, weight)


def total_over(values, axis):
    count = lax.axis_size(axis)
    step = 1
    while step < count:
        values = values + lax.ppermute(values, axis, [(i, i ^ step) for i in range(count)])
        step *= 2
    return values


def per_device(orbitals, potentials, local_potential, shifts):
    f32 = jnp.float32
    count, nz, strip, nx = orbitals.shape
    npot = potentials.shape[0]
    gy, bands = lax.axis_size("gy"), lax.axis_size("band")
    ny = strip * gy
    band, place = lax.axis_index("band"), lax.axis_index("gy")
    z_share, x_share = nz // bands, nx // gy

    def edge(rows):
        cut = [lax.slice_in_dim(f, *rows, axis=f.ndim - 2) for f in (orbitals, potentials, local_potential[None])]
        return jnp.concatenate(cut, axis=0)

    forward = [(i, i + 1) for i in range(gy - 1)]
    backward = [(b, a) for a, b in forward]
    low = lax.ppermute(edge((strip - HALO, strip)), "gy", forward)
    high = lax.ppermute(edge((0, HALO)), "gy", backward)
    low = jnp.pad(low, ((0, 0), (0, 0), (TILE - HALO, 0), (0, 0)))
    high = jnp.pad(high, ((0, 0), (0, 0), (0, TILE - HALO), (0, 0)))

    sums = total_over(project(orbitals, potentials), "gy")

    excess = shifts / spread_half
    s = 1.0 + excess
    less_one = excess * (2.0 + excess)
    fourth = 1.0 + 8.0 * s * s * less_one
    unit = 2.0 * spread_half
    constants = jnp.stack(
        [
            unit * s,
            unit * unit * less_one,
            unit**3 * s * less_one,
            -32.0 / (spread_half * unit**3) / fourth,
        ],
        axis=1,
    )
    edges = jnp.stack([place == 0, place == gy - 1]).astype(jnp.int32)

    sine_z = sine_values(nz)
    paired = bands == 4
    if paired:
        orders = [[b, b ^ 1] + ([2, 3] if b < 2 else [1, 0]) for b in range(bands)]
    else:
        orders = [list(range(bands))] * bands
    by_band = []
    for order in orders:
        index = np.concatenate([np.arange(z_share) + z_share * o for o in order])
        by_band.append(two_parts(np.kron(sine_z[index], np.eye(TILE))))
    z_table = lax.dynamic_index_in_dim(jnp.asarray(np.stack(by_band)), band, 0, keepdims=False)
    near = np.eye(nx, k=1) + np.eye(nx, k=-1)
    tables = (z_table, jnp.asarray(two_parts(sine_values(nx))), jnp.asarray(near, jnp.bfloat16))
    y_table = jnp.asarray(two_parts(sine_values(ny)))

    z_index = band * z_share + jnp.arange(z_share, dtype=jnp.int32)
    x_index = place * x_share + jnp.arange(x_share, dtype=jnp.int32)
    weight = coulomb(z_index, x_index, jnp.arange(ny, dtype=jnp.int32), (nz, nx, ny))

    outs = []
    for p in range(npot):
        mine, partner, far = stencil(
            p, 1, 0, strip, 4, sums, constants, edges, tables,
            (orbitals, potentials, local_potential), (low, high),
        )
        share = mine.shape[2]
        if paired:
            far = far + lax.ppermute(far, "band", [(0, 1), (3, 2)])
            back = lax.ppermute(far, "band", [(1, 2), (2, 1)])
            mine = mine + back[..., :share]
            partner = partner + back[..., share:]
            total = mine + lax.ppermute(partner, "band", [(0, 1), (1, 0), (2, 3), (3, 2)])
        else:
            joined = jnp.concatenate([mine, partner, far], axis=2)
            total = lax.psum_scatter(joined, "band", scatter_dimension=2, tiled=True)
        spread = total.reshape(gy, x_share, -1)
        received = lax.all_to_all(spread, "gy", split_axis=0, concat_axis=0, tiled=True)
        if paired:
            outs.append(finish(received, y_table, weight))
        else:
            terms = received.reshape(gy, x_share, z_share, strip)
            table = jnp.asarray(sine_values(ny), f32).reshape(gy, strip, ny)
            value = jnp.einsum("sjky,sym->kjm", terms, table, precision=lax.Precision.HIGHEST)
            outs.append(value * weight)
    return jnp.stack(outs)


def solution(mesh):
    placed = (
        P("band", None, "gy", None),
        P(None, None, "gy", None),
        P(None, "gy", None),
        P("band"),
    )
    return jax.shard_map(
        per_device,
        mesh=mesh,
        in_specs=placed,
        out_specs=P(None, "band", "gy", None),
        check_vma=False,
    )
```

```python
import functools

import jax
import jax.numpy as jnp
import numpy as np
from jax import lax
from jax.experimental import pallas as pl
from jax.experimental.pallas import tpu as pltpu
from jax.sharding import PartitionSpec as P

SWEEPS = 3
HALO = SWEEPS
TILE = 8
LANES = 128

spread_half = 3.5
screening = 0.25


def sine_values(length):
    index = np.arange(1, length + 1)
    phase = index[:, None] * index[None, :] % (2 * (length + 1))
    return np.sqrt(2.0 / (length + 1)) * np.sin(np.pi * phase / (length + 1))


def two_parts(values):
    whole = np.asarray(values, np.float32)
    high = whole.astype(jnp.bfloat16)
    low = (whole - high.astype(np.float32)).astype(jnp.bfloat16)
    return np.stack([high, low])


def split(value):
    high = value.astype(jnp.bfloat16)
    low = (value - high.astype(jnp.float32)).astype(jnp.bfloat16)
    return high, low


def product(a, b, contract):
    dims = (contract, ((), ()))
    dot = functools.partial(lax.dot_general, dimension_numbers=dims, preferred_element_type=jnp.float32)
    return dot(a[0], b[0]) + dot(a[1], b[0]) + dot(a[0], b[1])


def coulomb(z_index, x_index, y_index, sizes):
    nz, nx, ny = sizes
    wave_z = jnp.pi * (z_index.astype(jnp.float32) + 1.0) / (nz + 1)
    wave_x = jnp.pi * (x_index.astype(jnp.float32) + 1.0) / (nx + 1)
    wave_y = jnp.pi * (y_index.astype(jnp.float32) + 1.0) / (ny + 1)
    total = (
        wave_z[:, None, None] * wave_z[:, None, None]
        + wave_x[None, :, None] * wave_x[None, :, None]
    )
    total = total + wave_y[None, None, :] * wave_y[None, None, :] + screening
    return jnp.sqrt(4.0 * jnp.pi / total)


def project_kernel(orbitals, potentials, earlier, sums):
    count, planes, rows, width = orbitals.shape
    npot = potentials.shape[0]
    halves = width // LANES

    @pl.when(pl.program_id(0) == 0)
    def _():
        sums[...] = jnp.zeros_like(sums)

    def fold(value):
        return jnp.sum(value.reshape(rows // TILE, TILE, LANES), axis=0)

    def body(z, _):
        for half in range(halves):
            lanes = slice(half * LANES, (half + 1) * LANES)
            potential = [potentials[p, z, :, lanes] for p in range(npot)]
            for n in range(count):
                value = orbitals[n, z, :, lanes]
                square = value * value
                for p in range(npot):
                    sums[p * count + n] += fold(potential[p] * square)
                sums[npot * count + n] += fold(square)
        return 0

    lax.fori_loop(0, planes, body, 0)

    @pl.when(pl.program_id(0) == pl.num_programs(0) - 1)
    def _():
        sums[:, 0, :] = jnp.sum(sums[...], axis=1)


def project(orbitals, potentials, earlier):
    count, planes, rows, width = orbitals.shape
    npot = potentials.shape[0]
    step = 4
    total = (npot + 1) * count
    sums = pl.pallas_call(
        project_kernel,
        grid=(planes // step,),
        in_specs=[
            pl.BlockSpec((count, step, rows, width), lambda i: (0, i, 0, 0)),
            pl.BlockSpec((npot, step, rows, width), lambda i: (0, i, 0, 0)),
            pl.BlockSpec(memory_space=pl.ANY),
        ],
        out_specs=pl.BlockSpec((total, TILE, LANES), lambda i: (0, 0, 0)),
        out_shape=jax.ShapeDtypeStruct((total, TILE, LANES), jnp.float32),
        compiler_params=pltpu.CompilerParams(vmem_limit_bytes=60 << 20),
    )(orbitals, potentials, earlier)
    return sums[:, 0, :]


def edges_kernel(orbitals, potentials, local, first, last, tiles, sems):
    fields = []
    for source in (orbitals, potentials):
        fields += [source.at[i] for i in range(source.shape[0])]
    fields.append(local)
    planes, rows, width = local.shape
    copies = []
    for side, begin in enumerate((0, rows - TILE)):
        for i, field in enumerate(fields):
            copy = pltpu.make_async_copy(
                field.at[:, pl.ds(begin, TILE), :], tiles.at[side, i], sems.at[side, i]
            )
            copy.start()
            copies.append(copy)
    for copy in copies:
        copy.wait()
    for side, (out, begin) in enumerate(((first, 0), (last, TILE - HALO))):
        for i in range(len(fields)):
            for z in range(planes):
                out[i, z * HALO:(z + 1) * HALO, :] = tiles[side, i, z, begin:begin + HALO, :]


def pack_edges(orbitals, potentials, local):
    planes, _, width = local.shape
    fields = orbitals.shape[0] + potentials.shape[0] + 1
    vmem = pl.BlockSpec(memory_space=pltpu.VMEM)
    edge = jax.ShapeDtypeStruct((fields, planes * HALO, width), jnp.float32)
    return pl.pallas_call(
        edges_kernel,
        in_specs=[pl.BlockSpec(memory_space=pl.ANY)] * 3,
        out_specs=[vmem] * 2,
        out_shape=[edge] * 2,
        scratch_shapes=[
            pltpu.VMEM((2, fields, planes, TILE, width), jnp.float32),
            pltpu.SemaphoreType.DMA((2, fields)),
        ],
        compiler_params=pltpu.CompilerParams(vmem_limit_bytes=60 << 20),
    )(orbitals, potentials, local)


def stencil_kernel(
    geometry,
    coefficients, constants, place_index, z_tables, x_table,
    orbitals, potentials, local, low, high,
    mine, partner, far,
    orb, pot, loc, src, one, two, density, spectrum, low_rows, high_rows, z_table, table_sem, sems,
):
    pots, count, start, rows, strip, group = geometry
    npot = len(pots)
    planes = local.shape[0]
    width = local.shape[2]
    halves = width // LANES
    padded = rows + 2 * TILE
    wide = rows + TILE
    steps = planes // group
    f32 = jnp.float32
    begin, end = max(start - TILE, 0), min(start + rows + TILE, strip)
    place = begin - (start - TILE)
    need_low, need_high = start < TILE, start + rows + TILE > strip
    all_pots = low.shape[0] - count - 1
    packed = ((low, low_rows, TILE - HALO, need_low), (high, high_rows, padded - TILE, need_high))

    def pieces(kind, index, act):
        source, target, halo, sem = {
            "orb": (orbitals, orb, 0, 0), "pot": (potentials, pot, count, count), "loc": (local, loc, None, count + npot),
        }[kind]
        if kind == "loc":
            field, into, row, slot = source, lambda half: target.at[half], count + all_pots, sem
        elif kind == "pot":
            field, into, row, slot = source.at[pots[index]], lambda half: target.at[half, index], halo + pots[index], sem + index
        else:
            field, into, row, slot = source.at[index], lambda half: target.at[half, index], index, index
        for half in range(halves):
            lanes = pl.ds(half * LANES, LANES)
            copies = [(field.at[:, pl.ds(begin, end - begin), lanes], into(half).at[:, pl.ds(place, end - begin), :])]
            for sent, held, begin_row, needed in packed:
                if needed:
                    copies.append((sent.at[row, :, lanes], held.at[half, row]))
            for i, (a, b) in enumerate(copies):
                act(pltpu.make_async_copy(a, b, sems.at[slot, half, i]))
        if act is end_copy:
            for sent, held, begin_row, needed in packed:
                if needed:
                    for half in range(halves):
                        value = held[half, row]
                        for z in range(planes):
                            into(half)[z, begin_row:begin_row + HALO, :] = value[z * HALO:(z + 1) * HALO]

    def begin_copy(copy):
        copy.start()

    def end_copy(copy):
        copy.wait()

    pieces("loc", 0, begin_copy)
    for p in range(npot):
        pieces("pot", p, begin_copy)
    for n in range(count):
        pieces("orb", n, begin_copy)
    band = place_index[2]
    table_copy = pltpu.make_async_copy(z_tables.at[band], z_table, table_sem)
    table_copy.start()

    for field in (src, one, two):
        for p in range(npot):
            for half in range(halves):
                for z in (0, planes + 1):
                    field[half, p, z] = jnp.zeros(field.shape[3:], f32)

    def empty(z, _):
        for half in range(halves):
            for p in range(npot):
                density[half, p, z] = jnp.zeros((rows, LANES), f32)
        return 0

    lax.fori_loop(0, planes, empty, 0)
    first_edge = (place_index[0] == 1) if start == 0 else None
    last_edge = (place_index[1] == 1) if start + rows == strip else None

    pieces("loc", 0, end_copy)

    def weights(z, _):
        for half in range(halves):
            loc[half, z] = 1.0 - 2.0 * loc[half, z]
        return 0

    lax.fori_loop(0, planes, weights, 0)
    for p in range(npot):
        pieces("pot", p, end_copy)

    def cut(size):
        most = 3 * TILE if size % (3 * TILE) == 0 else 2 * TILE
        return [(r, min(most, size - r)) for r in range(0, size, most)]

    def sides(center):
        lane = lax.broadcasted_iota(jnp.int32, center[0].shape, 1)
        down = [pltpu.roll(c, 1, 1) for c in center]
        up = [pltpu.roll(c, LANES - 1, 1) for c in center]
        zero = jnp.zeros_like(center[0])
        down = [jnp.where(lane == 0, before, now) for before, now in zip([zero] + down[:-1], down)]
        up = [jnp.where(lane == LANES - 1, after, now) for after, now in zip(up[1:] + [zero], up)]
        return [a + b for a, b in zip(down, up)]

    def apply(field, offset, size, loc_offset, finish, step):
        z0 = step * group
        for r, length in cut(size):
            def load(p, i, shift):
                return [field[h, p, z0 + i + 1, pl.ds(offset + r + shift, length), :] for h in range(halves)]

            before = [load(p, -1, 0) for p in range(npot)]
            center = [load(p, 0, 0) for p in range(npot)]
            beside = [sides(c) for c in center]
            for i in range(group):
                after = [load(p, i + 1, 0) for p in range(npot)]
                beside_after = [sides(c) for c in after] if i + 1 < group else None
                total = []
                for p in range(npot):
                    under, over = load(p, i, -1), load(p, i, 1)
                    total.append([
                        (before[p][h] + after[p][h]) + (under[h] + over[h]) + beside[p][h] for h in range(halves)
                    ])
                for h in range(halves):
                    weight = loc[h, z0 + i, pl.ds(loc_offset + r, length), :]
                    finish(h, z0 + i, r, length, [t[h] for t in total], [c[h] for c in center], weight)
                before, center, beside = center, after, beside_after

    def clear(field, where, row, size):
        if where is not None:
            @pl.when(where)
            def _():
                for h in range(halves):
                    for p in range(npot):
                        field[h, p, :, pl.ds(row, size), :] = jnp.zeros((planes + 2, size, LANES), f32)

    def orbital(n, _):
        pieces("orb", n, end_copy)

        alpha, beta, scale = (constants[n, i] for i in range(3))
        factor = [coefficients[pots[p] * count + n] for p in range(npot)]

        def source(step):
            for i in range(group):
                z = step * group + i
                for h in range(halves):
                    value = orb[h, n, z]
                    for p in range(npot):
                        src[h, p, z + 1] = (pot[h, p, z] - factor[p]) * value

        def finish_one(h, z, r, length, total, center, weight):
            weight = weight + alpha
            for p in range(npot):
                one[h, p, z + 1, pl.ds(r, length), :] = total[p] + weight * center[p]

        def finish_two(h, z, r, length, total, center, weight):
            for p in range(npot):
                two[h, p, z + 1, pl.ds(r, length), :] = total[p] + weight * center[p]

        def finish_three(h, z, r, length, total, center, weight):
            value = orb[h, n, z, pl.ds(TILE + r, length), :] * scale
            for p in range(npot):
                third = total[p] + weight * center[p] + beta * one[h, p, z + 1, pl.ds(2 + r, length), :]
                density[h, p, z, pl.ds(r, length), :] += third * value

        applies = [
            source,
            functools.partial(apply, src, TILE - 2, wide, TILE - 2, finish_one),
            functools.partial(apply, one, 1, wide, TILE - 1, finish_two),
            functools.partial(apply, two, 1, rows, TILE, finish_three),
        ]
        for position, work in enumerate(applies):
            def body(step, _, work=work):
                work(step)
                return 0

            lax.fori_loop(0, steps, body, 0)
            if position == 1:
                clear(one, first_edge, 0, 2)
                clear(one, last_edge, rows + 2, 2)
            if position == 2:
                clear(two, first_edge, 0, 1)
                clear(two, last_edge, rows + 1, 1)
        return 0

    lax.fori_loop(0, count, orbital, 0)

    table_copy.wait()
    z_parts = (z_table[0], z_table[1])
    x_parts = (x_table[0], x_table[1])
    share = mine.shape[1] // npot
    block = min(share, 2 * LANES)
    for p in range(npot):
        for tile in range(rows // TILE):
            span = pl.ds(tile * TILE, TILE)
            value = jnp.concatenate(
                [density[h, p, :, span, :].reshape(planes * TILE, LANES) for h in range(halves)], axis=-1
            )
            value = product(z_parts, split(value), ((1,), (0,)))
            spectrum[:, span, :] = value.reshape(planes, TILE, width)
        for piece in range(planes * rows // block):
            at = piece * block
            value = spectrum[at // rows:(at + block) // rows].reshape(block, width)
            value = product(x_parts, split(value), ((1,), (1,)))
            for out, low_end, high_end in ((mine, 0, share), (partner, share, 2 * share)):
                if low_end <= at < high_end:
                    out[:, p * share + at - low_end:p * share + at - low_end + block] = value
            if at >= 2 * share:
                part, at = divmod(at - 2 * share, share)
                column = (part * npot + p) * share + at
                far[:, column:column + block] = value


def stencil(pots, start, rows, group, coefficients, constants, edges, tables, fields, halos):
    orbitals, potentials, local = fields
    count, planes, strip, width = orbitals.shape
    halves = width // LANES
    npot = len(pots)
    padded = rows + 2 * TILE
    share = planes * rows // 4
    geometry = (pots, count, start, rows, strip, group)
    vmem = pl.BlockSpec(memory_space=pltpu.VMEM)
    smem = pl.BlockSpec(memory_space=pltpu.SMEM)
    anywhere = pl.BlockSpec(memory_space=pl.ANY)
    f32 = jnp.float32
    return pl.pallas_call(
        functools.partial(stencil_kernel, geometry),
        in_specs=[smem, smem, smem, anywhere, vmem] + [anywhere] * 5,
        out_specs=[vmem] * 3,
        out_shape=[
            jax.ShapeDtypeStruct((width, npot * share), f32),
            jax.ShapeDtypeStruct((width, npot * share), f32),
            jax.ShapeDtypeStruct((width, npot * 2 * share), f32),
        ],
        scratch_shapes=[
            pltpu.VMEM((halves, count, planes, padded, LANES), f32),
            pltpu.VMEM((halves, npot, planes, padded, LANES), f32),
            pltpu.VMEM((halves, planes, padded, LANES), f32),
            pltpu.VMEM((halves, npot, planes + 2, padded, LANES), f32),
            pltpu.VMEM((halves, npot, planes + 2, padded, LANES), f32),
            pltpu.VMEM((halves, npot, planes + 2, padded, LANES), f32),
            pltpu.VMEM((halves, npot, planes, rows, LANES), f32),
            pltpu.VMEM((planes, rows, width), f32),
            pltpu.VMEM((halves, *halos[0].shape[:2], LANES), f32),
            pltpu.VMEM((halves, *halos[0].shape[:2], LANES), f32),
            pltpu.VMEM(tables[0].shape[1:], jnp.bfloat16),
            pltpu.SemaphoreType.DMA(()),
            pltpu.SemaphoreType.DMA((1 + npot + count, halves, 3)),
        ],
        compiler_params=pltpu.CompilerParams(vmem_limit_bytes=60 << 20),
        cost_estimate=pl.CostEstimate(flops=1 << 34, bytes_accessed=64 << 20, transcendentals=0),
    )(coefficients, constants, edges, *tables, orbitals, potentials, local, *halos)


def finish_kernel(received, table, weight, out):
    parts, x_share, lanes = received.shape
    z_share = out.shape[0]
    strip = lanes // z_share
    table_parts = (table[0], table[1])
    lane = lax.broadcasted_iota(jnp.int32, (x_share, LANES), 1)
    lower = lane < strip
    for pair in range(z_share // 2):
        columns = slice(pair * LANES, (pair + 1) * LANES)
        blocks = [received[i, :, columns] for i in range(parts)]
        rolled = [pltpu.roll(b, strip, 1) for b in blocks]
        even = [jnp.where(lower, blocks[i], rolled[i + 1]) for i in range(0, parts, 2)]
        odd = [jnp.where(lower, rolled[i], blocks[i + 1]) for i in range(0, parts, 2)]
        both = jnp.concatenate([jnp.concatenate(even, axis=-1), jnp.concatenate(odd, axis=-1)], axis=0)
        value = product(split(both), table_parts, ((1,), (0,)))
        out[2 * pair] = value[:x_share] * weight[2 * pair]
        out[2 * pair + 1] = value[x_share:] * weight[2 * pair + 1]


def finish(received, table, weight):
    vmem = pl.BlockSpec(memory_space=pltpu.VMEM)
    return pl.pallas_call(
        finish_kernel,
        in_specs=[vmem] * 3,
        out_specs=vmem,
        out_shape=jax.ShapeDtypeStruct(weight.shape, jnp.float32),
        compiler_params=pltpu.CompilerParams(vmem_limit_bytes=40 << 20),
    )(received, table, weight)


def total_over(values, axis):
    count = lax.axis_size(axis)
    step = 1
    while step < count:
        values = values + lax.ppermute(values, axis, [(i, i ^ step) for i in range(count)])
        step *= 2
    return values


def per_device(orbitals, potentials, local_potential, shifts):
    f32 = jnp.float32
    count, nz, strip, nx = orbitals.shape
    npot = potentials.shape[0]
    gy, bands = lax.axis_size("gy"), lax.axis_size("band")
    ny = strip * gy
    band, place = lax.axis_index("band"), lax.axis_index("gy")
    z_share, x_share = nz // bands, nx // gy

    first, last = pack_edges(orbitals, potentials, local_potential)
    forward = [(i, i + 1) for i in range(gy - 1)]
    backward = [(b, a) for a, b in forward]
    halos = (lax.ppermute(last, "gy", forward), lax.ppermute(first, "gy", backward))
    sums = total_over(project(orbitals, potentials, first), "gy")
    fields = (orbitals, potentials, local_potential)
    totals = jnp.sum(sums, axis=1).reshape(npot + 1, count)
    coefficients = (totals[:npot] / totals[npot]).reshape(-1)

    excess = shifts / spread_half
    s = 1.0 + excess
    less_one = excess * (2.0 + excess)
    fourth = 1.0 + 8.0 * s * s * less_one
    unit = 2.0 * spread_half
    constants = jnp.stack([unit * s, unit * unit * less_one, -32.0 / (spread_half * unit**3) / fourth], axis=1)
    edges = jnp.stack([(place == 0).astype(jnp.int32), (place == gy - 1).astype(jnp.int32), band])

    sine_z = sine_values(nz)
    paired = bands == 4
    if paired:
        orders = [[b, b ^ 1] + ([2, 3] if b < 2 else [1, 0]) for b in range(bands)]
    else:
        orders = [list(range(bands))] * bands
    by_band = []
    for order in orders:
        index = np.concatenate([np.arange(z_share) + z_share * o for o in order])
        by_band.append(two_parts(np.kron(sine_z[index], np.eye(TILE))))
    z_table = jnp.asarray(np.stack(by_band))
    tables = (z_table, jnp.asarray(two_parts(sine_values(nx))))
    z_index = band * z_share + jnp.arange(z_share, dtype=jnp.int32)
    x_index = place * x_share + jnp.arange(x_share, dtype=jnp.int32)
    weight = coulomb(z_index, x_index, jnp.arange(ny, dtype=jnp.int32), (nz, nx, ny))

    sine_y = sine_values(ny)
    y_table = jnp.asarray(two_parts(sine_y))
    outs = []
    for p in range(npot):
        mine, partner, far = stencil(
            (p,), 0, strip, 16, coefficients, constants, edges, tables, fields, halos
        )
        share = mine.shape[1]
        if paired:
            inward = lax.ppermute(far, "band", [(0, 1), (3, 2)])
            swapped = lax.ppermute(partner, "band", [(0, 1), (1, 0), (2, 3), (3, 2)])
            close = far[:, :share] + inward[:, :share]
            distant = far[:, share:] + inward[:, share:]
            close = lax.ppermute(close, "band", [(1, 2), (2, 1)])
            distant = lax.ppermute(distant, "band", [(1, 3), (2, 0)])
            total = mine + swapped + (close + distant)
        else:
            joined = jnp.concatenate([mine, partner, far], axis=1)
            total = lax.psum_scatter(joined, "band", scatter_dimension=1, tiled=True)
        spread = total.reshape(gy, x_share, -1)
        received = lax.all_to_all(spread, "gy", split_axis=0, concat_axis=0, tiled=True)
        if paired and 2 * strip == LANES:
            outs.append(finish(received, y_table, weight))
        else:
            terms = received.reshape(gy, x_share, z_share, strip)
            table = jnp.asarray(sine_y, f32).reshape(gy, strip, ny)
            value = jnp.einsum("sjky,sym->kjm", terms, table, precision=lax.Precision.HIGHEST)
            outs.append(value * weight)
    return jnp.stack(outs)


def solution(mesh):
    placed = (
        P("band", None, "gy", None),
        P(None, None, "gy", None),
        P(None, "gy", None),
        P("band"),
    )
    return jax.shard_map(
        per_device,
        mesh=mesh,
        in_specs=placed,
        out_specs=P(None, "band", "gy", None),
        check_vma=False,
    )
```

```python
import functools

import jax
import jax.numpy as jnp
import numpy as np
from jax import lax
from jax.experimental import pallas as pl
from jax.experimental.pallas import tpu as pltpu
from jax.sharding import PartitionSpec as P

SWEEPS = 3
HALO = SWEEPS
TILE = 8
LANES = 128

spread_half = 3.5
screening = 0.25


def sine_values(length):
    index = np.arange(1, length + 1)
    phase = index[:, None] * index[None, :] % (2 * (length + 1))
    return np.sqrt(2.0 / (length + 1)) * np.sin(np.pi * phase / (length + 1))


def two_parts(values):
    whole = np.asarray(values, np.float32)
    high = whole.astype(jnp.bfloat16)
    low = (whole - high.astype(np.float32)).astype(jnp.bfloat16)
    return np.stack([high, low])


def split(value):
    high = value.astype(jnp.bfloat16)
    low = (value - high.astype(jnp.float32)).astype(jnp.bfloat16)
    return high, low


def product(a, b, contract):
    dims = (contract, ((), ()))
    dot = functools.partial(lax.dot_general, dimension_numbers=dims, preferred_element_type=jnp.float32)
    return dot(a[0], b[0]) + dot(a[1], b[0]) + dot(a[0], b[1])


def coulomb(z_index, x_index, y_index, sizes):
    nz, nx, ny = sizes
    wave_z = jnp.pi * (z_index.astype(jnp.float32) + 1.0) / (nz + 1)
    wave_x = jnp.pi * (x_index.astype(jnp.float32) + 1.0) / (nx + 1)
    wave_y = jnp.pi * (y_index.astype(jnp.float32) + 1.0) / (ny + 1)
    total = (
        wave_z[:, None, None] * wave_z[:, None, None]
        + wave_x[None, :, None] * wave_x[None, :, None]
    )
    total = total + wave_y[None, None, :] * wave_y[None, None, :] + screening
    return jnp.sqrt(4.0 * jnp.pi / total)


def two_products(value, matrix):
    high, low = split(value)
    dot = functools.partial(jnp.dot, preferred_element_type=jnp.float32)
    return dot(high, matrix) + dot(low, matrix)


def project_kernel(orbitals, potentials, earlier, later, out, sums):
    count, planes, rows, width = orbitals.shape
    npot = potentials.shape[0]
    halves = width // LANES

    @pl.when(pl.program_id(0) == 0)
    def _():
        sums[...] = jnp.zeros_like(sums)

    def fold(value):
        return jnp.sum(value.reshape(rows // TILE, TILE, LANES), axis=0)

    def body(z, _):
        for half in range(halves):
            lanes = slice(half * LANES, (half + 1) * LANES)
            potential = [potentials[p, z, :, lanes] for p in range(npot)]
            for n in range(count):
                value = orbitals[n, z, :, lanes]
                square = value * value
                for p in range(npot):
                    sums[p * count + n] += fold(potential[p] * square)
                sums[npot * count + n] += fold(square)
        return 0

    lax.fori_loop(0, planes, body, 0)

    @pl.when(pl.program_id(0) == pl.num_programs(0) - 1)
    def _():
        out[...] = jnp.sum(sums[...], axis=1)


def project(orbitals, potentials, earlier, later):
    count, planes, rows, width = orbitals.shape
    npot = potentials.shape[0]
    step = TILE
    total = (npot + 1) * count
    sums = pl.pallas_call(
        project_kernel,
        grid=(planes // step,),
        in_specs=[
            pl.BlockSpec((count, step, rows, width), lambda i: (0, i, 0, 0)),
            pl.BlockSpec((npot, step, rows, width), lambda i: (0, i, 0, 0)),
            pl.BlockSpec(memory_space=pl.ANY),
            pl.BlockSpec(memory_space=pl.ANY),
        ],
        out_specs=pl.BlockSpec((total, LANES), lambda i: (0, 0)),
        out_shape=jax.ShapeDtypeStruct((total, LANES), jnp.float32),
        scratch_shapes=[pltpu.VMEM((total, TILE, LANES), jnp.float32)],
        compiler_params=pltpu.CompilerParams(vmem_limit_bytes=60 << 20),
    )(orbitals, potentials, earlier, later)
    return sums


def reorder_kernel(*refs):
    order, fields = refs[0], refs[1:]
    sources, targets = fields[:len(fields) // 2], fields[len(fields) // 2:]
    width = order.shape[0]
    joined = jnp.concatenate([source[...].reshape(-1, width) for source in sources], axis=0)
    value = two_products(joined, order[...])
    at = 0
    for target in targets:
        size = target.size // width
        part = value[at:at + size]
        if target is targets[-1]:
            part = 1.0 - 2.0 * part
        target[...] = part.reshape(target.shape)
        at += size


def reorder(fields, order):
    planes, _, width = fields[-1].shape
    step = TILE

    def spec(field):
        lead = field.ndim - 3
        shape = (*field.shape[:lead], step, *field.shape[lead + 1:])
        return pl.BlockSpec(shape, lambda i: (0,) * lead + (i, 0, 0))

    specs = [spec(field) for field in fields]
    size = sum(field.size for field in fields)
    return pl.pallas_call(
        reorder_kernel,
        grid=(planes // step,),
        in_specs=[pl.BlockSpec((width, width), lambda i: (0, 0))] + specs,
        out_specs=specs,
        out_shape=[jax.ShapeDtypeStruct(v.shape, jnp.float32) for v in fields],
        compiler_params=pltpu.CompilerParams(vmem_limit_bytes=60 << 20),
        cost_estimate=pl.CostEstimate(flops=4 * size * width, bytes_accessed=8 * size, transcendentals=0),
    )(order, *fields)


def edges_kernel(orbitals, potentials, local, order, first, last, tiles, packed, sems):
    fields = []
    for source in (orbitals, potentials):
        fields += [source.at[i] for i in range(source.shape[0])]
    fields.append(local)
    planes, rows, width = local.shape
    copies = []
    for side, begin in enumerate((0, rows - TILE)):
        for i, field in enumerate(fields):
            copy = pltpu.make_async_copy(
                field.at[:, pl.ds(begin, TILE), :], tiles.at[side, i], sems.at[side, i]
            )
            copy.start()
            copies.append(copy)
    for copy in copies:
        copy.wait()
    size = planes * HALO
    for side, (out, begin) in enumerate(((first, 0), (last, TILE - HALO))):
        for i in range(len(fields)):
            for z in range(planes):
                packed[i * size + z * HALO:i * size + (z + 1) * HALO, :] = tiles[side, i, z, begin:begin + HALO, :]
        value = two_products(packed[...], order[...])
        diagonal = size * (len(fields) - 1)
        out[0:len(fields) - 1] = value[:diagonal].reshape(len(fields) - 1, size, width)
        out[len(fields) - 1] = 1.0 - 2.0 * value[diagonal:]


def pack_edges(orbitals, potentials, local, order):
    planes, _, width = local.shape
    fields = orbitals.shape[0] + potentials.shape[0] + 1
    vmem = pl.BlockSpec(memory_space=pltpu.VMEM)
    edge = jax.ShapeDtypeStruct((fields, planes * HALO, width), jnp.float32)
    return pl.pallas_call(
        edges_kernel,
        in_specs=[pl.BlockSpec(memory_space=pl.ANY)] * 3 + [vmem],
        out_specs=[vmem] * 2,
        out_shape=[edge] * 2,
        scratch_shapes=[
            pltpu.VMEM((2, fields, planes, TILE, width), jnp.float32),
            pltpu.VMEM((fields * planes * HALO, width), jnp.float32),
            pltpu.SemaphoreType.DMA((2, fields)),
        ],
        compiler_params=pltpu.CompilerParams(vmem_limit_bytes=60 << 20),
    )(orbitals, potentials, local, order)


def stencil_kernel(
    geometry,
    coefficients, constants, place_index, z_tables, x_tables,
    orbitals, potentials, local, low, high, *refs,
):
    outs = refs[geometry[-1]:-15]
    (orb, pot, loc, src, one, two, density, spectrum, low_rows, high_rows, z_table, x_table, table_sem, x_sem, sems) = refs[-15:]
    pots, count, start, rows, strip, group, _ = geometry
    npot = len(pots)
    planes = local.shape[0]
    width = local.shape[2]
    halves = width // LANES
    padded = rows + 2 * TILE
    wide = rows + TILE
    steps = planes // group
    f32 = jnp.float32
    begin, end = max(start - TILE, 0), min(start + rows + TILE, strip)
    place = begin - (start - TILE)
    need_low, need_high = start < TILE, start + rows + TILE > strip
    all_pots = low.shape[0] - count - 1
    packed = ((low, low_rows, TILE - HALO, need_low), (high, high_rows, padded - TILE, need_high))

    def pieces(kind, index, act):
        source, target, halo, sem = {
            "orb": (orbitals, orb, 0, 0), "pot": (potentials, pot, count, count), "loc": (local, loc, None, count + npot),
        }[kind]
        if kind == "loc":
            field, into, row, slot = source, lambda half: target.at[half], count + all_pots, sem
        elif kind == "pot":
            field, into, row, slot = source.at[pots[index]], lambda half: target.at[half, index], halo + pots[index], sem + index
        else:
            field, into, row, slot = source.at[index], lambda half: target.at[half, index], index, index
        for half in range(halves):
            lanes = pl.ds(half * LANES, LANES)
            copies = [(field.at[:, pl.ds(begin, end - begin), lanes], into(half).at[:, pl.ds(place, end - begin), :])]
            for sent, held, begin_row, needed in packed:
                if needed:
                    copies.append((sent.at[row, :, lanes], held.at[half, row]))
            for i, (a, b) in enumerate(copies):
                act(pltpu.make_async_copy(a, b, sems.at[slot, half, i]))
        if act is end_copy:
            for sent, held, begin_row, needed in packed:
                if needed:
                    for half in range(halves):
                        value = held[half, row]
                        for z in range(planes):
                            into(half)[z, begin_row:begin_row + HALO, :] = value[z * HALO:(z + 1) * HALO]

    def begin_copy(copy):
        copy.start()

    def end_copy(copy):
        copy.wait()

    pieces("loc", 0, begin_copy)
    for p in range(npot):
        pieces("pot", p, begin_copy)
    for n in range(count):
        pieces("orb", n, begin_copy)
    band = place_index[2]
    table_copy = pltpu.make_async_copy(z_tables.at[band], z_table, table_sem)
    table_copy.start()
    x_copy = pltpu.make_async_copy(x_tables, x_table, x_sem)
    x_copy.start()

    for field in (src, one, two):
        for p in range(npot):
            for half in range(halves):
                for z in (0, planes + 1):
                    field[half, p, z] = jnp.zeros(field.shape[3:], f32)

    def empty(z, _):
        for half in range(halves):
            for p in range(npot):
                density[half, p, z] = jnp.zeros((rows, LANES), f32)
        return 0

    lax.fori_loop(0, planes, empty, 0)
    first_edge = (place_index[0] == 1) if start == 0 else None
    last_edge = (place_index[1] == 1) if start + rows == strip else None

    pieces("loc", 0, end_copy)

    for p in range(npot):
        pieces("pot", p, end_copy)

    def cut(size):
        most = 3 * TILE if size % (3 * TILE) == 0 else 2 * TILE
        return [(r, min(most, size - r)) for r in range(0, size, most)]

    def sides(center):
        even, odd = center
        lane = lax.broadcasted_iota(jnp.int32, even.shape, 1)
        zero = jnp.zeros_like(even)
        down = jnp.where(lane == 0, zero, pltpu.roll(odd, 1, 1))
        up = jnp.where(lane == LANES - 1, zero, pltpu.roll(even, LANES - 1, 1))
        return [odd + down, even + up]

    def apply(field, offset, size, loc_offset, finish, step):
        z0 = step * group
        for r, length in cut(size):
            def load(p, i, shift):
                return [field[h, p, z0 + i + 1, pl.ds(offset + r + shift, length), :] for h in range(halves)]

            before = [load(p, -1, 0) for p in range(npot)]
            center = [load(p, 0, 0) for p in range(npot)]
            beside = [sides(c) for c in center]
            for i in range(group):
                after = [load(p, i + 1, 0) for p in range(npot)]
                beside_after = [sides(c) for c in after] if i + 1 < group else None
                total = []
                for p in range(npot):
                    under, over = load(p, i, -1), load(p, i, 1)
                    total.append([
                        (before[p][h] + after[p][h]) + (under[h] + over[h]) + beside[p][h] for h in range(halves)
                    ])
                for h in range(halves):
                    weight = loc[h, z0 + i, pl.ds(loc_offset + r, length), :]
                    finish(h, z0 + i, r, length, [t[h] for t in total], [c[h] for c in center], weight)
                before, center, beside = center, after, beside_after

    def clear(field, where, row, size):
        if where is not None:
            @pl.when(where)
            def _():
                for h in range(halves):
                    for p in range(npot):
                        field[h, p, :, pl.ds(row, size), :] = jnp.zeros((planes + 2, size, LANES), f32)

    def orbital(n, _):
        pieces("orb", n, end_copy)

        alpha, beta, scale = (constants[n, i] for i in range(3))
        factor = [coefficients[pots[p] * count + n] for p in range(npot)]

        def source(step):
            for i in range(group):
                z = step * group + i
                for h in range(halves):
                    value = orb[h, n, z]
                    for p in range(npot):
                        src[h, p, z + 1] = (pot[h, p, z] - factor[p]) * value

        def finish_one(h, z, r, length, total, center, weight):
            weight = weight + alpha
            for p in range(npot):
                one[h, p, z + 1, pl.ds(r, length), :] = total[p] + weight * center[p]

        def finish_two(h, z, r, length, total, center, weight):
            for p in range(npot):
                two[h, p, z + 1, pl.ds(r, length), :] = total[p] + weight * center[p]

        def finish_three(h, z, r, length, total, center, weight):
            value = orb[h, n, z, pl.ds(TILE + r, length), :] * scale
            for p in range(npot):
                third = total[p] + weight * center[p] + beta * one[h, p, z + 1, pl.ds(2 + r, length), :]
                density[h, p, z, pl.ds(r, length), :] += third * value

        applies = [
            source,
            functools.partial(apply, src, TILE - 2, wide, TILE - 2, finish_one),
            functools.partial(apply, one, 1, wide, TILE - 1, finish_two),
            functools.partial(apply, two, 1, rows, TILE, finish_three),
        ]
        for position, work in enumerate(applies):
            def body(step, _, work=work):
                work(step)
                return 0

            lax.fori_loop(0, steps, body, 0)
            if position == 1:
                clear(one, first_edge, 0, 2)
                clear(one, last_edge, rows + 2, 2)
            if position == 2:
                clear(two, first_edge, 0, 1)
                clear(two, last_edge, rows + 1, 1)
        return 0

    lax.fori_loop(0, count, orbital, 0)

    table_copy.wait()
    x_copy.wait()
    z_parts = (z_table[0], z_table[1])
    x_parts = (x_table[0], x_table[1])
    share = outs[0].shape[2]
    block = min(share, 2 * LANES)
    places = [(out, i) for out in outs for i in range(out.shape[0])]
    for tile in range(rows // TILE):
        span = pl.ds(tile * TILE, TILE)
        value = jnp.concatenate(
            [density[h, 0, :, span, :].reshape(planes * TILE, LANES) for h in range(halves)], axis=-1
        )
        value = product(z_parts, split(value), ((1,), (0,)))
        spectrum[:, span, :] = value.reshape(planes, TILE, width)
    for piece in range(planes * rows // block):
        at = piece * block
        value = spectrum[at // rows:(at + block) // rows].reshape(block, width)
        value = product(x_parts, split(value), ((1,), (1,)))
        out, i = places[at // share]
        out[i, :, at % share:at % share + block] = value


def stencil(pots, start, rows, group, coefficients, constants, edges, tables, fields, halos, blocks, earlier=()):
    orbitals, potentials, local = fields
    count, planes, strip, width = orbitals.shape
    halves = width // LANES
    npot = len(pots)
    padded = rows + 2 * TILE
    share = planes * rows // sum(blocks)
    geometry = (pots, count, start, rows, strip, group, len(earlier))
    vmem = pl.BlockSpec(memory_space=pltpu.VMEM)
    smem = pl.BlockSpec(memory_space=pltpu.SMEM)
    anywhere = pl.BlockSpec(memory_space=pl.ANY)
    f32 = jnp.float32
    return pl.pallas_call(
        functools.partial(stencil_kernel, geometry),
        in_specs=[smem, smem, smem, anywhere, anywhere] + [anywhere] * (5 + len(earlier)),
        out_specs=[vmem] * len(blocks),
        out_shape=[jax.ShapeDtypeStruct((i, width, share), f32) for i in blocks],
        scratch_shapes=[
            pltpu.VMEM((halves, count, planes, padded, LANES), f32),
            pltpu.VMEM((halves, npot, planes, padded, LANES), f32),
            pltpu.VMEM((halves, planes, padded, LANES), f32),
            pltpu.VMEM((halves, npot, planes + 2, padded, LANES), f32),
            pltpu.VMEM((halves, npot, planes + 2, padded, LANES), f32),
            pltpu.VMEM((halves, npot, planes + 2, padded, LANES), f32),
            pltpu.VMEM((halves, npot, planes, rows, LANES), f32),
            pltpu.VMEM((planes, rows, width), f32),
            pltpu.VMEM((halves, *halos[0].shape[:2], LANES), f32),
            pltpu.VMEM((halves, *halos[0].shape[:2], LANES), f32),
            pltpu.VMEM(tables[0].shape[1:], jnp.bfloat16),
            pltpu.VMEM(tables[1].shape, jnp.bfloat16),
            pltpu.SemaphoreType.DMA(()),
            pltpu.SemaphoreType.DMA(()),
            pltpu.SemaphoreType.DMA((1 + npot + count, halves, 3)),
        ],
        compiler_params=pltpu.CompilerParams(vmem_limit_bytes=63 << 20),
        cost_estimate=pl.CostEstimate(flops=1 << 34, bytes_accessed=64 << 20, transcendentals=0),
    )(coefficients, constants, edges, *tables, orbitals, potentials, local, *halos, *earlier)


def finish_kernel(pieces, received, table, weight, *refs):
    out = refs[-1]
    parts, x_share, _ = received.shape
    z_share = out.shape[1]
    strip = sum(pieces)
    table_parts = (table[0], table[1])
    lane = lax.broadcasted_iota(jnp.int32, (x_share, LANES), 1)
    joined = []
    for k in range(z_share):
        columns = []
        for first in range(0, parts, LANES // strip):
            value, target = None, 0
            for source in range(first, first + LANES // strip):
                base = 0
                for rows in pieces:
                    at = base + k * rows
                    tile = received[source, :, at // LANES * LANES:at // LANES * LANES + LANES]
                    turn = (target - at) % LANES
                    tile = pltpu.roll(tile, turn, 1) if turn else tile
                    value = tile if value is None else jnp.where(lane < target, value, tile)
                    base += z_share * rows
                    target += rows
            columns.append(value)
        joined.append(jnp.concatenate(columns, axis=-1))
    value = product(split(jnp.concatenate(joined, axis=0)), table_parts, ((1,), (0,)))
    for k in range(z_share):
        out[0, k] = value[k * x_share:(k + 1) * x_share] * weight[k]


def finish(p, npot, pieces, received, table, weight, result):
    whole = [received, table, weight]
    specs = [pl.BlockSpec(v.shape, lambda i, n=v.ndim: (0,) * n) for v in whole]
    return pl.pallas_call(
        functools.partial(finish_kernel, pieces),
        grid=(1,),
        in_specs=specs + ([] if result is None else [pl.BlockSpec(memory_space=pl.ANY)]),
        out_specs=pl.BlockSpec((1, *weight.shape), lambda i: (p, 0, 0, 0)),
        out_shape=jax.ShapeDtypeStruct((npot, *weight.shape), jnp.float32),
        input_output_aliases={} if result is None else {3: 0},
        compiler_params=pltpu.CompilerParams(vmem_limit_bytes=40 << 20),
    )(*whole, *([] if result is None else [result]))


def total_over(values, axis):
    count = lax.axis_size(axis)
    step = 1
    while step < count:
        values = values + lax.ppermute(values, axis, [(i, i ^ step) for i in range(count)])
        step *= 2
    return values


def per_device(orbitals, potentials, local_potential, shifts):
    f32 = jnp.float32
    count, nz, strip, nx = orbitals.shape
    npot = potentials.shape[0]
    gy, bands = lax.axis_size("gy"), lax.axis_size("band")
    ny = strip * gy
    band, place = lax.axis_index("band"), lax.axis_index("gy")
    z_share, x_share = nz // bands, nx // gy

    along_x = np.concatenate([np.arange(0, nx, 2), np.arange(1, nx, 2)])
    order = jnp.asarray(np.eye(nx)[:, along_x], jnp.bfloat16)
    first, last = pack_edges(orbitals, potentials, local_potential, order)
    forward = [(i, i + 1) for i in range(gy - 1)]
    backward = [(b, a) for a, b in forward]
    halos = (lax.ppermute(last, "gy", forward), lax.ppermute(first, "gy", backward))
    sums = total_over(project(orbitals, potentials, first, last), "gy")
    fields = reorder((orbitals, potentials, local_potential), order)
    totals = jnp.sum(sums, axis=1).reshape(npot + 1, count)
    coefficients = (totals[:npot] / totals[npot]).reshape(-1)

    excess = shifts / spread_half
    s = 1.0 + excess
    less_one = excess * (2.0 + excess)
    fourth = 1.0 + 8.0 * s * s * less_one
    unit = 2.0 * spread_half
    constants = jnp.stack([unit * s, unit * unit * less_one, -32.0 / (spread_half * unit**3) / fourth], axis=1)
    place_index = jnp.stack([(place == 0).astype(jnp.int32), (place == gy - 1).astype(jnp.int32), band])

    sine_z = sine_values(nz)
    paired = bands == 4
    plain = list(range(bands))
    near_first = [[b, b ^ 1] + ([2, 3] if b < 2 else [1, 0]) for b in range(bands)] if paired else [plain] * bands

    def z_tables(orders):
        by_band = []
        for order in orders:
            index = np.concatenate([np.arange(z_share) + z_share * o for o in order])
            by_band.append(two_parts(np.kron(sine_z[index], np.eye(TILE))))
        return jnp.asarray(np.stack(by_band))

    x_table = jnp.asarray(two_parts(sine_values(nx)[:, along_x]))
    z_index = band * z_share + jnp.arange(z_share, dtype=jnp.int32)
    x_index = place * x_share + jnp.arange(x_share, dtype=jnp.int32)
    weight = coulomb(z_index, x_index, jnp.arange(ny, dtype=jnp.int32), (nz, nx, ny))

    sine_y = sine_values(ny)
    y_table = jnp.asarray(two_parts(sine_y))
    def exchange(total):
        spread = total.reshape(gy, x_share, -1)
        return lax.all_to_all(spread, "gy", split_axis=0, concat_axis=0, tiled=True)

    def share_out(p, start, rows, blocks, earlier=()):
        tables = (z_tables(near_first if paired else [plain] * bands), x_table)
        return stencil(
            (p,), start, rows, 16, coefficients, constants, place_index, tables, fields, halos, blocks, earlier
        )

    def inward(far):
        sent = lax.ppermute(far, "band", [(0, 1), (3, 2)])
        return far[:1] + sent[:1], far[1:] + sent[1:]

    def outward(partner, close, distant):
        return (
            lax.ppermute(close, "band", [(1, 2), (2, 1)]),
            lax.ppermute(distant, "band", [(1, 3), (2, 0)]),
            lax.ppermute(partner, "band", [(0, 1), (1, 0), (2, 3), (3, 2)]),
        )

    def add_up(mine, got):
        return (mine + got[2] + (got[0] + got[1]))[0]

    if paired and 2 * strip == LANES:
        result = None
        for p in range(npot):
            mine, partner, far = share_out(p, 0, strip, (1, 1, 2))
            far = far + lax.ppermute(far, "band", [(0, 1), (3, 2)])
            total = add_up(mine, outward(partner, far[:1], far[1:]))
            result = finish(p, npot, (strip,), exchange(total), y_table, weight, result)
        return result
    outs = []
    for p in range(npot):
        total = lax.psum_scatter(share_out(p, 0, strip, (bands,))[0], "band", scatter_dimension=0, tiled=True)
        terms = exchange(total).reshape(gy, x_share, z_share, strip)
        table = jnp.asarray(sine_y, f32).reshape(gy, strip, ny)
        value = jnp.einsum("sjky,sym->kjm", terms, table, precision=lax.Precision.HIGHEST)
        outs.append(value * weight)
    return jnp.stack(outs)


def solution(mesh):
    placed = (
        P("band", None, "gy", None),
        P(None, None, "gy", None),
        P(None, "gy", None),
        P("band"),
    )
    return jax.shard_map(
        per_device,
        mesh=mesh,
        in_specs=placed,
        out_specs=P(None, "band", "gy", None),
        check_vma=False,
    )
```

```python
import functools

import jax
import jax.numpy as jnp
import numpy as np
from jax import lax
from jax.experimental import pallas as pl
from jax.experimental.pallas import tpu as pltpu
from jax.sharding import PartitionSpec as P

SWEEPS = 3
HALO = SWEEPS
TILE = 8
LANES = 128

spread_half = 3.5
screening = 0.25


def sine_values(length):
    index = np.arange(1, length + 1)
    phase = index[:, None] * index[None, :] % (2 * (length + 1))
    return np.sqrt(2.0 / (length + 1)) * np.sin(np.pi * phase / (length + 1))


def two_parts(values):
    whole = np.asarray(values, np.float32)
    high = whole.astype(jnp.bfloat16)
    low = (whole - high.astype(np.float32)).astype(jnp.bfloat16)
    return np.stack([high, low])


def split(value):
    high = value.astype(jnp.bfloat16)
    low = (value - high.astype(jnp.float32)).astype(jnp.bfloat16)
    return high, low


def product(a, b, contract):
    dims = (contract, ((), ()))
    dot = functools.partial(lax.dot_general, dimension_numbers=dims, preferred_element_type=jnp.float32)
    return dot(a[0], b[0]) + dot(a[1], b[0]) + dot(a[0], b[1])


def coulomb(z_index, x_index, y_index, sizes):
    nz, nx, ny = sizes
    wave_z = jnp.pi * (z_index.astype(jnp.float32) + 1.0) / (nz + 1)
    wave_x = jnp.pi * (x_index.astype(jnp.float32) + 1.0) / (nx + 1)
    wave_y = jnp.pi * (y_index.astype(jnp.float32) + 1.0) / (ny + 1)
    total = (
        wave_z[:, None, None] * wave_z[:, None, None]
        + wave_x[None, :, None] * wave_x[None, :, None]
    )
    total = total + wave_y[None, None, :] * wave_y[None, None, :] + screening
    return jnp.sqrt(4.0 * jnp.pi / total)


def two_products(value, matrix):
    high, low = split(value)
    dot = functools.partial(jnp.dot, preferred_element_type=jnp.float32)
    return dot(high, matrix) + dot(low, matrix)


def prepare_kernel(orbitals, potentials, local, order, earlier, later, out, *refs):
    targets, sums = refs[:-1], refs[-1]
    count, planes, rows, width = orbitals.shape
    npot = potentials.shape[0]
    halves = width // LANES

    @pl.when(pl.program_id(0) == 0)
    def _():
        sums[...] = jnp.zeros_like(sums)

    joined = jnp.concatenate([f[...].reshape(-1, width) for f in (orbitals, potentials, local)], axis=0)
    value = two_products(joined, order[...])
    at = 0
    for target in targets:
        size = target.size // width
        part = value[at:at + size]
        if target is targets[-1]:
            part = 1.0 - 2.0 * part
        target[...] = part.reshape(target.shape)
        at += size

    def fold(value):
        return jnp.sum(value.reshape(rows // TILE, TILE, LANES), axis=0)

    def body(z, _):
        for half in range(halves):
            lanes = slice(half * LANES, (half + 1) * LANES)
            potential = [potentials[p, z, :, lanes] for p in range(npot)]
            for n in range(count):
                value = orbitals[n, z, :, lanes]
                square = value * value
                for p in range(npot):
                    sums[p * count + n] += fold(potential[p] * square)
                sums[npot * count + n] += fold(square)
        return 0

    lax.fori_loop(0, planes, body, 0)

    @pl.when(pl.program_id(0) == pl.num_programs(0) - 1)
    def _():
        out[...] = jnp.sum(sums[...], axis=1)


def prepare(fields, order, earlier, later):
    orbitals, potentials, local = fields
    planes, _, width = local.shape
    step = TILE
    total = (potentials.shape[0] + 1) * orbitals.shape[0]

    def spec(field):
        lead = field.ndim - 3
        shape = (*field.shape[:lead], step, *field.shape[lead + 1:])
        return pl.BlockSpec(shape, lambda i: (0,) * lead + (i, 0, 0))

    specs = [spec(field) for field in fields]
    anywhere = pl.BlockSpec(memory_space=pl.ANY)
    sums, *ordered = pl.pallas_call(
        prepare_kernel,
        grid=(planes // step,),
        in_specs=specs + [pl.BlockSpec((width, width), lambda i: (0, 0)), anywhere, anywhere],
        out_specs=[pl.BlockSpec((total, LANES), lambda i: (0, 0))] + specs,
        out_shape=[jax.ShapeDtypeStruct((total, LANES), jnp.float32)]
        + [jax.ShapeDtypeStruct(f.shape, jnp.float32) for f in fields],
        scratch_shapes=[pltpu.VMEM((total, TILE, LANES), jnp.float32)],
        compiler_params=pltpu.CompilerParams(vmem_limit_bytes=60 << 20),
    )(*fields, order, earlier, later)
    return sums, ordered


def edges_kernel(orbitals, potentials, local, order, first, last, tiles, packed, sems):
    fields = []
    for source in (orbitals, potentials):
        fields += [source.at[i] for i in range(source.shape[0])]
    fields.append(local)
    planes, rows, width = local.shape
    copies = []
    for side, begin in enumerate((0, rows - TILE)):
        for i, field in enumerate(fields):
            copy = pltpu.make_async_copy(
                field.at[:, pl.ds(begin, TILE), :], tiles.at[side, i], sems.at[side, i]
            )
            copy.start()
            copies.append(copy)
    for copy in copies:
        copy.wait()
    size = planes * HALO
    for side, (out, begin) in enumerate(((first, 0), (last, TILE - HALO))):
        for i in range(len(fields)):
            for z in range(planes):
                packed[i * size + z * HALO:i * size + (z + 1) * HALO, :] = tiles[side, i, z, begin:begin + HALO, :]
        value = two_products(packed[...], order[...])
        diagonal = size * (len(fields) - 1)
        out[0:len(fields) - 1] = value[:diagonal].reshape(len(fields) - 1, size, width)
        out[len(fields) - 1] = 1.0 - 2.0 * value[diagonal:]


def pack_edges(orbitals, potentials, local, order):
    planes, _, width = local.shape
    fields = orbitals.shape[0] + potentials.shape[0] + 1
    vmem = pl.BlockSpec(memory_space=pltpu.VMEM)
    edge = jax.ShapeDtypeStruct((fields, planes * HALO, width), jnp.float32)
    return pl.pallas_call(
        edges_kernel,
        in_specs=[pl.BlockSpec(memory_space=pl.ANY)] * 3 + [vmem],
        out_specs=[vmem] * 2,
        out_shape=[edge] * 2,
        scratch_shapes=[
            pltpu.VMEM((2, fields, planes, TILE, width), jnp.float32),
            pltpu.VMEM((fields * planes * HALO, width), jnp.float32),
            pltpu.SemaphoreType.DMA((2, fields)),
        ],
        compiler_params=pltpu.CompilerParams(vmem_limit_bytes=60 << 20),
    )(orbitals, potentials, local, order)


def stencil_kernel(
    geometry,
    coefficients, constants, place_index, z_tables, x_tables,
    orbitals, potentials, local, low, high, *refs,
):
    outs = refs[geometry[-1]:-15]
    (orb, pot, loc, src, one, two, density, spectrum, low_rows, high_rows, z_table, x_table, table_sem, x_sem, sems) = refs[-15:]
    pots, count, start, rows, strip, group, _ = geometry
    npot = len(pots)
    planes = local.shape[0]
    width = local.shape[2]
    halves = width // LANES
    padded = rows + 2 * TILE
    wide = rows + TILE
    steps = planes // group
    f32 = jnp.float32
    begin, end = max(start - TILE, 0), min(start + rows + TILE, strip)
    place = begin - (start - TILE)
    need_low, need_high = start < TILE, start + rows + TILE > strip
    all_pots = low.shape[0] - count - 1
    packed = ((low, low_rows, TILE - HALO, need_low), (high, high_rows, padded - TILE, need_high))

    def pieces(kind, index, act):
        source, target, halo, sem = {
            "orb": (orbitals, orb, 0, 0), "pot": (potentials, pot, count, count), "loc": (local, loc, None, count + npot),
        }[kind]
        if kind == "loc":
            field, into, row, slot = source, lambda half: target.at[half], count + all_pots, sem
        elif kind == "pot":
            field, into, row, slot = source.at[pots[index]], lambda half: target.at[half, index], halo + pots[index], sem + index
        else:
            field, into, row, slot = source.at[index], lambda half: target.at[half, index], index, index
        for half in range(halves):
            lanes = pl.ds(half * LANES, LANES)
            copies = [(field.at[:, pl.ds(begin, end - begin), lanes], into(half).at[:, pl.ds(place, end - begin), :])]
            for sent, held, begin_row, needed in packed:
                if needed:
                    copies.append((sent.at[row, :, lanes], held.at[half, row]))
            for i, (a, b) in enumerate(copies):
                act(pltpu.make_async_copy(a, b, sems.at[slot, half, i]))
        if act is end_copy:
            for sent, held, begin_row, needed in packed:
                if needed:
                    for half in range(halves):
                        value = held[half, row]
                        for z in range(planes):
                            into(half)[z, begin_row:begin_row + HALO, :] = value[z * HALO:(z + 1) * HALO]

    def begin_copy(copy):
        copy.start()

    def end_copy(copy):
        copy.wait()

    pieces("loc", 0, begin_copy)
    for p in range(npot):
        pieces("pot", p, begin_copy)
    for n in range(count):
        pieces("orb", n, begin_copy)
    band = place_index[2]
    table_copy = pltpu.make_async_copy(z_tables.at[band], z_table, table_sem)
    table_copy.start()
    x_copy = pltpu.make_async_copy(x_tables, x_table, x_sem)
    x_copy.start()

    for field in (src, one, two):
        for p in range(npot):
            for half in range(halves):
                for z in (0, planes + 1):
                    field[half, p, z] = jnp.zeros(field.shape[3:], f32)

    def empty(z, _):
        for half in range(halves):
            for p in range(npot):
                density[half, p, z] = jnp.zeros((rows, LANES), f32)
        return 0

    lax.fori_loop(0, planes, empty, 0)
    first_edge = (place_index[0] == 1) if start == 0 else None
    last_edge = (place_index[1] == 1) if start + rows == strip else None

    pieces("loc", 0, end_copy)

    for p in range(npot):
        pieces("pot", p, end_copy)

    def cut(size):
        most = 3 * TILE if size % (3 * TILE) == 0 else 2 * TILE
        return [(r, min(most, size - r)) for r in range(0, size, most)]

    def sides(center):
        even, odd = center
        lane = lax.broadcasted_iota(jnp.int32, even.shape, 1)
        zero = jnp.zeros_like(even)
        down = jnp.where(lane == 0, zero, pltpu.roll(odd, 1, 1))
        up = jnp.where(lane == LANES - 1, zero, pltpu.roll(even, LANES - 1, 1))
        return [odd + down, even + up]

    def apply(field, offset, size, loc_offset, finish, step):
        z0 = step * group
        for r, length in cut(size):
            def load(p, i, shift):
                return [field[h, p, z0 + i + 1, pl.ds(offset + r + shift, length), :] for h in range(halves)]

            before = [load(p, -1, 0) for p in range(npot)]
            center = [load(p, 0, 0) for p in range(npot)]
            beside = [sides(c) for c in center]
            for i in range(group):
                after = [load(p, i + 1, 0) for p in range(npot)]
                beside_after = [sides(c) for c in after] if i + 1 < group else None
                total = []
                for p in range(npot):
                    under, over = load(p, i, -1), load(p, i, 1)
                    total.append([
                        (before[p][h] + after[p][h]) + (under[h] + over[h]) + beside[p][h] for h in range(halves)
                    ])
                for h in range(halves):
                    weight = loc[h, z0 + i, pl.ds(loc_offset + r, length), :]
                    finish(h, z0 + i, r, length, [t[h] for t in total], [c[h] for c in center], weight)
                before, center, beside = center, after, beside_after

    def clear(field, where, row, size):
        if where is not None:
            @pl.when(where)
            def _():
                for h in range(halves):
                    for p in range(npot):
                        field[h, p, :, pl.ds(row, size), :] = jnp.zeros((planes + 2, size, LANES), f32)

    def orbital(n, _):
        pieces("orb", n, end_copy)

        alpha, beta, scale = (constants[n, i] for i in range(3))
        factor = [coefficients[pots[p] * count + n] for p in range(npot)]

        def source(step):
            for i in range(group):
                z = step * group + i
                for h in range(halves):
                    value = orb[h, n, z]
                    for p in range(npot):
                        src[h, p, z + 1] = (pot[h, p, z] - factor[p]) * value

        def finish_one(h, z, r, length, total, center, weight):
            weight = weight + alpha
            for p in range(npot):
                one[h, p, z + 1, pl.ds(r, length), :] = total[p] + weight * center[p]

        def finish_two(h, z, r, length, total, center, weight):
            for p in range(npot):
                two[h, p, z + 1, pl.ds(r, length), :] = total[p] + weight * center[p]

        def finish_three(h, z, r, length, total, center, weight):
            value = orb[h, n, z, pl.ds(TILE + r, length), :] * scale
            for p in range(npot):
                third = total[p] + weight * center[p] + beta * one[h, p, z + 1, pl.ds(2 + r, length), :]
                density[h, p, z, pl.ds(r, length), :] += third * value

        applies = [
            source,
            functools.partial(apply, src, TILE - 2, wide, TILE - 2, finish_one),
            functools.partial(apply, one, 1, wide, TILE - 1, finish_two),
            functools.partial(apply, two, 1, rows, TILE, finish_three),
        ]
        for position, work in enumerate(applies):
            def body(step, _, work=work):
                work(step)
                return 0

            lax.fori_loop(0, steps, body, 0)
            if position == 1:
                clear(one, first_edge, 0, 2)
                clear(one, last_edge, rows + 2, 2)
            if position == 2:
                clear(two, first_edge, 0, 1)
                clear(two, last_edge, rows + 1, 1)
        return 0

    lax.fori_loop(0, count, orbital, 0)

    table_copy.wait()
    x_copy.wait()
    z_parts = (z_table[0], z_table[1])
    x_parts = (x_table[0], x_table[1])
    share = outs[0].shape[2]
    block = min(share, 2 * LANES)
    places = [(out, i) for out in outs for i in range(out.shape[0])]
    for tile in range(rows // TILE):
        span = pl.ds(tile * TILE, TILE)
        value = jnp.concatenate(
            [density[h, 0, :, span, :].reshape(planes * TILE, LANES) for h in range(halves)], axis=-1
        )
        value = product(z_parts, split(value), ((1,), (0,)))
        spectrum[:, span, :] = value.reshape(planes, TILE, width)
    for piece in range(planes * rows // block):
        at = piece * block
        value = spectrum[at // rows:(at + block) // rows].reshape(block, width)
        value = product(x_parts, split(value), ((1,), (1,)))
        out, i = places[at // share]
        out[i, :, at % share:at % share + block] = value


def stencil(pots, start, rows, group, coefficients, constants, edges, tables, fields, halos, blocks, earlier=()):
    orbitals, potentials, local = fields
    count, planes, strip, width = orbitals.shape
    halves = width // LANES
    npot = len(pots)
    padded = rows + 2 * TILE
    share = planes * rows // sum(blocks)
    geometry = (pots, count, start, rows, strip, group, len(earlier))
    vmem = pl.BlockSpec(memory_space=pltpu.VMEM)
    smem = pl.BlockSpec(memory_space=pltpu.SMEM)
    anywhere = pl.BlockSpec(memory_space=pl.ANY)
    f32 = jnp.float32
    return pl.pallas_call(
        functools.partial(stencil_kernel, geometry),
        in_specs=[smem, smem, smem, anywhere, anywhere] + [anywhere] * (5 + len(earlier)),
        out_specs=[vmem] * len(blocks),
        out_shape=[jax.ShapeDtypeStruct((i, width, share), f32) for i in blocks],
        scratch_shapes=[
            pltpu.VMEM((halves, count, planes, padded, LANES), f32),
            pltpu.VMEM((halves, npot, planes, padded, LANES), f32),
            pltpu.VMEM((halves, planes, padded, LANES), f32),
            pltpu.VMEM((halves, npot, planes + 2, padded, LANES), f32),
            pltpu.VMEM((halves, npot, planes + 2, padded, LANES), f32),
            pltpu.VMEM((halves, npot, planes + 2, padded, LANES), f32),
            pltpu.VMEM((halves, npot, planes, rows, LANES), f32),
            pltpu.VMEM((planes, rows, width), f32),
            pltpu.VMEM((halves, *halos[0].shape[:2], LANES), f32),
            pltpu.VMEM((halves, *halos[0].shape[:2], LANES), f32),
            pltpu.VMEM(tables[0].shape[1:], jnp.bfloat16),
            pltpu.VMEM(tables[1].shape, jnp.bfloat16),
            pltpu.SemaphoreType.DMA(()),
            pltpu.SemaphoreType.DMA(()),
            pltpu.SemaphoreType.DMA((1 + npot + count, halves, 3)),
        ],
        compiler_params=pltpu.CompilerParams(vmem_limit_bytes=63 << 20),
        cost_estimate=pl.CostEstimate(flops=1 << 34, bytes_accessed=64 << 20, transcendentals=0),
    )(coefficients, constants, edges, *tables, orbitals, potentials, local, *halos, *earlier)


def finish_kernel(pieces, received, table, weight, *refs):
    out = refs[-1]
    parts, x_share, _ = received.shape
    z_share = out.shape[1]
    strip = sum(pieces)
    table_parts = (table[0], table[1])
    lane = lax.broadcasted_iota(jnp.int32, (x_share, LANES), 1)
    joined = []
    for k in range(z_share):
        columns = []
        for first in range(0, parts, LANES // strip):
            value, target = None, 0
            for source in range(first, first + LANES // strip):
                base = 0
                for rows in pieces:
                    at = base + k * rows
                    tile = received[source, :, at // LANES * LANES:at // LANES * LANES + LANES]
                    turn = (target - at) % LANES
                    tile = pltpu.roll(tile, turn, 1) if turn else tile
                    value = tile if value is None else jnp.where(lane < target, value, tile)
                    base += z_share * rows
                    target += rows
            columns.append(value)
        joined.append(jnp.concatenate(columns, axis=-1))
    value = product(split(jnp.concatenate(joined, axis=0)), table_parts, ((1,), (0,)))
    for k in range(z_share):
        out[0, k] = value[k * x_share:(k + 1) * x_share] * weight[k]


def finish(p, npot, pieces, received, table, weight, result):
    whole = [received, table, weight]
    specs = [pl.BlockSpec(v.shape, lambda i, n=v.ndim: (0,) * n) for v in whole]
    return pl.pallas_call(
        functools.partial(finish_kernel, pieces),
        grid=(1,),
        in_specs=specs + ([] if result is None else [pl.BlockSpec(memory_space=pl.ANY)]),
        out_specs=pl.BlockSpec((1, *weight.shape), lambda i: (p, 0, 0, 0)),
        out_shape=jax.ShapeDtypeStruct((npot, *weight.shape), jnp.float32),
        input_output_aliases={} if result is None else {3: 0},
        compiler_params=pltpu.CompilerParams(vmem_limit_bytes=40 << 20),
    )(*whole, *([] if result is None else [result]))


def total_over(values, axis):
    count = lax.axis_size(axis)
    step = 1
    while step < count:
        values = values + lax.ppermute(values, axis, [(i, i ^ step) for i in range(count)])
        step *= 2
    return values


def per_device(orbitals, potentials, local_potential, shifts):
    f32 = jnp.float32
    count, nz, strip, nx = orbitals.shape
    npot = potentials.shape[0]
    gy, bands = lax.axis_size("gy"), lax.axis_size("band")
    ny = strip * gy
    band, place = lax.axis_index("band"), lax.axis_index("gy")
    z_share, x_share = nz // bands, nx // gy

    along_x = np.concatenate([np.arange(0, nx, 2), np.arange(1, nx, 2)])
    order = jnp.asarray(np.eye(nx)[:, along_x], jnp.bfloat16)
    first, last = pack_edges(orbitals, potentials, local_potential, order)
    forward = [(i, i + 1) for i in range(gy - 1)]
    backward = [(b, a) for a, b in forward]
    halos = (lax.ppermute(last, "gy", forward), lax.ppermute(first, "gy", backward))
    sums, fields = prepare((orbitals, potentials, local_potential), order, first, last)
    sums = total_over(sums, "gy")
    totals = jnp.sum(sums, axis=1).reshape(npot + 1, count)
    coefficients = (totals[:npot] / totals[npot]).reshape(-1)

    excess = shifts / spread_half
    s = 1.0 + excess
    less_one = excess * (2.0 + excess)
    fourth = 1.0 + 8.0 * s * s * less_one
    unit = 2.0 * spread_half
    constants = jnp.stack([unit * s, unit * unit * less_one, -32.0 / (spread_half * unit**3) / fourth], axis=1)
    place_index = jnp.stack([(place == 0).astype(jnp.int32), (place == gy - 1).astype(jnp.int32), band])

    sine_z = sine_values(nz)
    paired = bands == 4
    plain = list(range(bands))
    near_first = [[b, b ^ 1] + ([2, 3] if b < 2 else [1, 0]) for b in range(bands)] if paired else [plain] * bands

    def z_tables(orders):
        by_band = []
        for order in orders:
            index = np.concatenate([np.arange(z_share) + z_share * o for o in order])
            by_band.append(two_parts(np.kron(sine_z[index], np.eye(TILE))))
        return jnp.asarray(np.stack(by_band))

    x_table = jnp.asarray(two_parts(sine_values(nx)[:, along_x]))
    z_index = band * z_share + jnp.arange(z_share, dtype=jnp.int32)
    x_index = place * x_share + jnp.arange(x_share, dtype=jnp.int32)
    weight = coulomb(z_index, x_index, jnp.arange(ny, dtype=jnp.int32), (nz, nx, ny))

    sine_y = sine_values(ny)
    y_table = jnp.asarray(two_parts(sine_y))
    def exchange(total):
        spread = total.reshape(gy, x_share, -1)
        return lax.all_to_all(spread, "gy", split_axis=0, concat_axis=0, tiled=True)

    def share_out(p, start, rows, blocks, earlier=()):
        tables = (z_tables(near_first if paired else [plain] * bands), x_table)
        return stencil(
            (p,), start, rows, 32, coefficients, constants, place_index, tables, fields, halos, blocks, earlier
        )

    def inward(far):
        sent = lax.ppermute(far, "band", [(0, 1), (3, 2)])
        return far[:1] + sent[:1], far[1:] + sent[1:]

    def outward(partner, close, distant):
        return (
            lax.ppermute(close, "band", [(1, 2), (2, 1)]),
            lax.ppermute(distant, "band", [(1, 3), (2, 0)]),
            lax.ppermute(partner, "band", [(0, 1), (1, 0), (2, 3), (3, 2)]),
        )

    def add_up(mine, got):
        return (mine + got[2] + (got[0] + got[1]))[0]

    if paired and 2 * strip == LANES:
        result = None
        for p in range(npot):
            mine, partner, far = share_out(p, 0, strip, (1, 1, 2))
            far = far + lax.ppermute(far, "band", [(0, 1), (3, 2)])
            total = add_up(mine, outward(partner, far[:1], far[1:]))
            result = finish(p, npot, (strip,), exchange(total), y_table, weight, result)
        return result
    outs = []
    for p in range(npot):
        total = lax.psum_scatter(share_out(p, 0, strip, (bands,))[0], "band", scatter_dimension=0, tiled=True)
        terms = exchange(total).reshape(gy, x_share, z_share, strip)
        table = jnp.asarray(sine_y, f32).reshape(gy, strip, ny)
        value = jnp.einsum("sjky,sym->kjm", terms, table, precision=lax.Precision.HIGHEST)
        outs.append(value * weight)
    return jnp.stack(outs)


def solution(mesh):
    placed = (
        P("band", None, "gy", None),
        P(None, None, "gy", None),
        P(None, "gy", None),
        P("band"),
    )
    return jax.shard_map(
        per_device,
        mesh=mesh,
        in_specs=placed,
        out_specs=P(None, "band", "gy", None),
        check_vma=False,
    )
```
